32 devices in a mesh: energy: 2 (over y), kpt: 16 (over z, x, core).
Axes of the slice: x: 2, y: 2, z: 4, core: 2. Of those that a mesh axis runs over, the one named last changes fastest.
Arguments:
- left_table: bfloat16 [512, 4096], P('kpt'), may hold values from -6 to 6
- band_table: bfloat16 [512, 4096], P('kpt'), may hold values from -18.75 to 18.75
- band_multipole: int32 [512], P('kpt'), may hold values from 0 to 7
- radial_weight: float32 [8, 4096], replicated, may hold values from 0.25 to 4
- green_weight: float32 [1024], P(('energy', 'kpt')), parts along dimension 0, may hold values from 0.3 to 3
Outputs:
- kernel_cyclic: bfloat16 [1024, 512], P(('energy', 'kpt')), parts along dimension 0
The draws below stay inside these ranges and needn't reach their ends.
There are 2 independent parts, one for each index of `energy`. The reference program is written for one: setup_inputs(seed, part) draws one part's arguments, and reference() takes and returns one part's arrays. A program takes and returns all parts, laid end to end along the dimension named above; an argument that names none is the same for every part. Nothing has to cross between parts.
All inputs are finite; a program needn't handle non-finite values.
Results may differ from the reference program's by a relative error of at most 0.0049.
Values may be sent and summed in bfloat16 or wider, within the bound.
A program may use at most 128 MiB of HBM per device.

```python
import math
import jax
import jax.numpy as jnp
from jax import lax

R = 4096
LMAX = 8
NB = 2
ROW_DEV = 32
ROWS = 512
BAND = 512
N_KPT = 16


def radial_profile(head_value, tail_value):
    places = jnp.arange(R)
    return jnp.where(places < R // 4, head_value, tail_value).astype(jnp.float32)


def draw_left_table(key, part):
    values = jnp.clip(jax.random.normal(jax.random.fold_in(key, 11), (ROWS, R), jnp.float32), -6.0, 6.0)
    return (values * radial_profile(0.001, 1.0)[None, :]).astype(jnp.bfloat16)


def draw_band_table(key, part):
    values = jnp.clip(jax.random.normal(jax.random.fold_in(key, 23), (BAND, R), jnp.float32), -6.0, 6.0)
    return (values * radial_profile(3.125, 0.015625)[None, :]).astype(jnp.bfloat16)


def plant(entries, key, smallest, high):
    place = [jax.random.randint(jax.random.fold_in(key, axis), (), 0, length) for axis, length in enumerate(entries.shape)]
    widest = entries.shape.index(max(entries.shape))
    beside = place[:widest] + [(place[widest] + 1) % entries.shape[widest]] + place[widest + 1:]
    return entries.at[tuple(place)].set(smallest).at[tuple(beside)].set(high)


def shard_levels(stream_key, shape, cuts, low, largest):
    level, own = 1.0, jax.random.fold_in(stream_key, 6)
    for axis_at, parts in cuts:
        steps = jnp.exp(jax.random.uniform(jax.random.fold_in(own, axis_at), (parts,), jnp.float32, low / len(cuts), largest / len(cuts)))
        level = level * jnp.repeat(steps, shape[axis_at] // parts).reshape([-1 if axis == axis_at else 1 for axis in range(len(shape))])
    return level


def setup_inputs(seed: int = 0, part: int = 0) -> dict:
    key_list = jax.random.split(jax.random.key(seed), 6)
    part_splits = jax.random.split(jax.random.fold_in(key_list[5], part), 6)
    return {
        "left_table": draw_left_table(jax.random.fold_in(key_list[5], 71), part),
        "band_table": draw_band_table(jax.random.fold_in(key_list[5], 71), part),
        "band_multipole": plant(jax.random.randint(key_list[2], (BAND,), 0, LMAX), jax.random.fold_in(key_list[2], 1), 0, LMAX - 1).astype(jnp.int32),
        "radial_weight": jnp.clip(jnp.exp(jax.random.uniform(key_list[3], (LMAX, R), jnp.float32, math.log(0.25), math.log(4.0))), 0.25, 4.0),
        "green_weight": jnp.clip(jnp.exp(math.log(3.0) - 2.3025851 * jax.random.uniform(part_splits[4], (BAND,), jnp.float32) ** shard_levels(part_splits[4], (BAND,), ((0, 16),), -0.2, 0.2)), 0.3, 3.0),
    }


def reference(left_table, band_table, band_multipole, radial_weight, green_weight):
    picked = jnp.take(radial_weight, band_multipole, axis=0)
    weighted = (band_table.astype(jnp.float32) * picked * green_weight[:, None]).astype(jnp.bfloat16)
    weighted_full = weighted.astype(jnp.float32)
    row_blocks = left_table.reshape(N_KPT, ROW_DEV, R)

    def build_block(row_block):
        return jnp.dot(row_block.astype(jnp.float32), weighted_full.T, precision=lax.Precision.HIGHEST).astype(jnp.bfloat16)

    kernel = lax.map(build_block, row_blocks)
    kernel = kernel.reshape(N_KPT, N_KPT, NB, BAND).transpose(1, 0, 2, 3)
    return kernel.reshape(ROWS, BAND)
```

```python
import functools

import jax
import jax.numpy as jnp
from jax import lax
from jax.experimental import pallas as pl
from jax.experimental.pallas import tpu as pltpu
from jax.sharding import PartitionSpec as P

LMAX = 8
MESH = pl.DeviceIdType.MESH
CHUNKS = 4


def build_part(left_table, band_part):
    return lax.dot_general(
        left_table, band_part, (((1,), (1,)), ((), ())), preferred_element_type=jnp.float32
    ).astype(jnp.bfloat16)


def per_device(left_table, band_table, band_multipole, radial_weight, green_weight):
    group_size = lax.axis_size("kpt")
    row_count = left_table.shape[0]
    block_rows = row_count // group_size
    levels = lax.broadcasted_iota(jnp.int32, (1, LMAX), 1)
    onehot = (band_multipole[:, None] == levels).astype(jnp.float32)
    picked = jnp.dot(onehot, radial_weight, precision=lax.Precision.HIGHEST)
    weighted = (band_table.astype(jnp.float32) * picked * green_weight[:, None]).astype(
        jnp.bfloat16
    )
    gathered = lax.all_gather(weighted, "kpt", axis=0, tiled=True)
    band_total = gathered.shape[0]
    kernel_rows = build_part(left_table, gathered)
    shaped = kernel_rows.reshape(group_size, block_rows, band_total)
    relaid = lax.all_to_all(shaped, "kpt", split_axis=0, concat_axis=0, tiled=True)
    return relaid.reshape(row_count, band_total)


def grid_kernel(
    left, band, mult, radial, green, out,
    lbuf, bbuf, rbuf, info, infobuf, psend, precv, msg, outbuf,
    rsem, lsem, bsem, isem, psem, osem, lsend, bsend, isend, osend,
):
    e = lax.axis_index("energy")
    k = lax.axis_index("kpt")
    c, x, z = k % 2, (k // 2) % 2, k // 4
    half = lbuf.shape[1]
    step = half // CHUNKS
    rows = left.shape[0]
    own = k % 4

    barrier = pltpu.get_barrier_semaphore()
    for de in range(2):
        for dk in range(16):
            if de or dk:
                pl.semaphore_signal(
                    barrier, inc=1, device_id=((e + de) % 2, (k + dk) % 16), device_id_type=MESH
                )

    def cols(core, n):
        return pl.ds(pl.multiple_of(core * half + n * step, 128), step)

    def slot(i):
        return pl.ds(pl.multiple_of(i * rows, rows), rows)

    def at(n):
        return pl.ds(n * step, step)

    radial_copy = pltpu.make_async_copy(
        radial.at[:, pl.ds(pl.multiple_of(c * half, 128), half)], rbuf, rsem
    )
    radial_copy.start()
    for n in range(CHUNKS):
        pltpu.make_async_copy(
            left.at[:, cols(c, n)], lbuf.at[slot(own), at(n)], lsem.at[own, n]
        ).start()

    @pl.when(c == e)
    def _():
        for n in range(CHUNKS):
            pltpu.make_async_copy(
                band.at[:, cols(c, n)], bbuf.at[slot(z), at(n)], bsem.at[z, n]
            ).start()

    info[...] = jnp.zeros_like(info)
    info[0:1, 0:rows] = green[...]
    info[1:2, 0:rows] = mult[...].astype(jnp.float32)
    info[...] = pltpu.roll(info[...], z * rows, 1)

    pl.semaphore_wait(barrier, 31)

    sends = []
    for dz in range(4):
        for dc in range(2):
            target = (c, ((z + dz) % 4) * 4 + 2 * x + (c + dc) % 2)
            copy = pltpu.make_async_remote_copy(
                src_ref=info, dst_ref=infobuf.at[e, z], send_sem=isend.at[dz * 2 + dc],
                recv_sem=isem.at[e, z], device_id=target, device_id_type=MESH,
            )
            if dz or dc:
                copy.start()
                sends.append(copy)
            else:
                own_info = copy
    info_local = pltpu.make_async_copy(info, infobuf.at[e, z], isem.at[e, z])

    @pl.when(c == e)
    def _():
        info_local.start()

    @pl.when(c != e)
    def _():
        own_info.start()

    band_sends = []
    for n in range(CHUNKS):
        for i, (dx, dc) in enumerate(((1, 0), (1, 1), (0, 1))):
            core = (c + dc) % 2
            copy = pltpu.make_async_remote_copy(
                src_ref=left.at[:, cols(core, n)], dst_ref=lbuf.at[slot(own), at(n)],
                send_sem=lsend.at[i, n], recv_sem=lsem.at[own, n],
                device_id=(e, 4 * z + 2 * ((x + dx) % 2) + core), device_id_type=MESH,
            )
            copy.start()
            sends.append(copy)
        for i, (dz, dc) in enumerate(((1, 0), (1, 1), (2, 0), (2, 1), (3, 0), (3, 1), (0, 1))):
            core = (c + dc) % 2
            band_sends.append(
                pltpu.make_async_remote_copy(
                    src_ref=band.at[:, cols(core, n)], dst_ref=bbuf.at[slot(z), at(n)],
                    send_sem=bsend.at[i, n], recv_sem=bsem.at[z, n],
                    device_id=(e, ((z + dz) % 4) * 4 + 2 * x + core), device_id_type=MESH,
                )
            )

    @pl.when(c == e)
    def _():
        for copy in band_sends:
            copy.start()

    radial_copy.wait()
    whole = rbuf[...]
    high = whole.astype(jnp.bfloat16)
    rest = whole - high.astype(jnp.float32)
    middle = rest.astype(jnp.bfloat16)
    low = rest - middle.astype(jnp.float32)
    terms = jnp.concatenate(
        [high.astype(jnp.float32), middle.astype(jnp.float32), low, jnp.zeros_like(low)], axis=0
    ).astype(jnp.bfloat16)

    for energy in range(2):
        for zz in range(4):
            pltpu.make_async_copy(info, infobuf.at[energy, zz], isem.at[energy, zz]).wait()
    data = [infobuf[i, 0] + infobuf[i, 1] + infobuf[i, 2] + infobuf[i, 3] for i in range(2)]
    lanes = 4 * rows
    down = lax.broadcasted_iota(jnp.int32, (lanes, lanes), 0)
    across = lax.broadcasted_iota(jnp.int32, (lanes, lanes), 1)
    scale = [
        jnp.sum(jnp.where(down == across, data[i][0:1, :], 0.0), axis=1, keepdims=True)
        for i in range(2)
    ]
    first = c == 0
    mine = jnp.where(first, scale[0], scale[1])
    other = jnp.where(first, scale[1], scale[0])
    level = jnp.sum(jnp.where(down == across, data[0][1:2, :], 0.0), axis=1, keepdims=True)
    place = lax.broadcasted_iota(jnp.int32, (lanes, 4 * LMAX), 1)
    onehot = jnp.where(
        jnp.logical_and((place % LMAX).astype(jnp.float32) == level, place < 3 * LMAX), 1.0, 0.0
    ).astype(jnp.bfloat16)

    total = jnp.zeros((lanes, 2 * lanes), jnp.float32)
    for n in range(CHUNKS):
        picked = jnp.dot(
            onehot, terms[:, n * step:(n + 1) * step], preferred_element_type=jnp.float32
        )
        for i in range(4):
            pltpu.make_async_copy(
                lbuf.at[slot(i), at(n)], lbuf.at[slot(i), at(n)], lsem.at[i, n]
            ).wait()
            pltpu.make_async_copy(
                bbuf.at[slot(i), at(n)], bbuf.at[slot(i), at(n)], bsem.at[i, n]
            ).wait()
        product = bbuf[:, n * step:(n + 1) * step].astype(jnp.float32) * picked
        weighted = jnp.concatenate(
            [(product * other).astype(jnp.bfloat16), (product * mine).astype(jnp.bfloat16)], axis=0
        )
        total += lax.dot_general(
            lbuf[:, n * step:(n + 1) * step], weighted, (((1,), (1,)), ((), ())),
            preferred_element_type=jnp.float32,
        )

    psend[...] = total[:, :lanes]
    half_sum = pltpu.make_async_remote_copy(
        src_ref=psend, dst_ref=precv, send_sem=psem.at[0], recv_sem=psem.at[1],
        device_id=(e, 4 * z + 2 * x + (c + 1) % 2), device_id_type=MESH,
    )
    half_sum.start()
    block, pair = down // 8, down % 8
    order = jnp.where(across == (pair // 2) * rows + block * 2 + pair % 2, 1.0, 0.0).astype(
        jnp.bfloat16
    )
    half_sum.wait_recv()
    finished = (total[:, lanes:] + precv[...]).astype(jnp.bfloat16)
    cyclic = jnp.dot(order, finished, preferred_element_type=jnp.float32)
    msg[...] = cyclic.reshape(msg.shape)

    for dq in range(16):
        q = (k + dq) % 16
        copy = pltpu.make_async_remote_copy(
            src_ref=msg.at[q], dst_ref=outbuf.at[z, 2 * x + e], send_sem=osend.at[dq],
            recv_sem=osem.at[z, 2 * x + e], device_id=(c, q), device_id_type=MESH,
        )
        if dq:
            copy.start()
            sends.append(copy)
        else:
            own_out = copy
    out_local = pltpu.make_async_copy(msg.at[k], outbuf.at[z, 2 * x + e], osem.at[z, 2 * x + e])

    @pl.when(c == e)
    def _():
        out_local.start()

    @pl.when(c != e)
    def _():
        own_out.start()

    lane = lax.broadcasted_iota(jnp.int32, (8, lanes), 1) // rows
    for zz in range(4):
        for s in range(4):
            pltpu.make_async_copy(msg.at[0], outbuf.at[zz, s], osem.at[zz, s]).wait()
    for top in range(2):
        for tile in range(4):
            parts = []
            for zz in (2 * top, 2 * top + 1):
                whole_tile = jnp.zeros((8, lanes), jnp.float32)
                for s in range(4):
                    turned = outbuf[zz, s]
                    if (s - tile) % 4:
                        turned = pltpu.roll(turned, ((s - tile) % 4) * rows, 1)
                    whole_tile = jnp.where(lane == s, turned, whole_tile)
                parts.append(whole_tile)
            out[top * 16:(top + 1) * 16, tile * lanes:(tile + 1) * lanes] = jnp.concatenate(
                parts, axis=0
            ).astype(jnp.bfloat16)

    for copy in sends:
        copy.wait_send()
    half_sum.wait_send()

    @pl.when(c == e)
    def _():
        for copy in band_sends:
            copy.wait_send()

    @pl.when(c != e)
    def _():
        own_info.wait_send()
        own_out.wait_send()


def per_device_grid(left_table, band_table, band_multipole, radial_weight, green_weight):
    rows, points = left_table.shape
    lanes, half = 4 * rows, points // 2
    dma = pltpu.SemaphoreType.DMA
    any_space = pl.BlockSpec(memory_space=pl.ANY)
    vmem = pl.BlockSpec(memory_space=pltpu.VMEM)
    return pl.pallas_call(
        grid_kernel,
        out_shape=jax.ShapeDtypeStruct((rows, 16 * rows), jnp.bfloat16),
        in_specs=[any_space, any_space, vmem, any_space, vmem],
        out_specs=vmem,
        scratch_shapes=[
            pltpu.VMEM((lanes, half), jnp.bfloat16),
            pltpu.VMEM((lanes, half), jnp.bfloat16),
            pltpu.VMEM((LMAX, half), jnp.float32),
            pltpu.VMEM((8, lanes), jnp.float32),
            pltpu.VMEM((2, 4, 8, lanes), jnp.float32),
            pltpu.VMEM((lanes, lanes), jnp.float32),
            pltpu.VMEM((lanes, lanes), jnp.float32),
            pltpu.VMEM((16, 8, lanes), jnp.float32),
            pltpu.VMEM((4, 4, 8, lanes), jnp.float32),
            dma, dma((4, CHUNKS)), dma((4, CHUNKS)), dma((2, 4)), dma((2,)), dma((4, 4)),
            dma((3, CHUNKS)), dma((7, CHUNKS)), dma((8,)), dma((16,)),
        ],
        compiler_params=pltpu.CompilerParams(
            collective_id=0, has_side_effects=True, vmem_limit_bytes=32 * 1024 * 1024
        ),
    )(left_table, band_table, band_multipole.reshape(1, rows), radial_weight, green_weight.reshape(1, rows))


def solution(mesh):
    in_specs = (P("kpt", None), P("kpt", None), P("kpt"), P(), P(("energy", "kpt")))
    out_specs = P(("energy", "kpt"), None)

    def step(left_table, band_table, band_multipole, radial_weight, green_weight):
        small = (
            mesh.shape["energy"] == 2
            and mesh.shape["kpt"] == 16
            and left_table.shape == band_table.shape == (32, 4096)
        )
        body = per_device_grid if small else per_device
        return body(left_table, band_table, band_multipole, radial_weight, green_weight)

    return jax.shard_map(
        step, mesh=mesh, in_specs=in_specs, out_specs=out_specs, check_vma=False
    )
```

```python
import functools

import jax
import jax.numpy as jnp
from jax import lax
from jax.experimental import pallas as pl
from jax.experimental.pallas import tpu as pltpu
from jax.sharding import PartitionSpec as P

LMAX = 8
MESH = pl.DeviceIdType.MESH
CHUNKS = 4


def build_part(left_table, band_part):
    return lax.dot_general(
        left_table, band_part, (((1,), (1,)), ((), ())), preferred_element_type=jnp.float32
    ).astype(jnp.bfloat16)


def per_device(left_table, band_table, band_multipole, radial_weight, green_weight):
    group_size = lax.axis_size("kpt")
    row_count = left_table.shape[0]
    block_rows = row_count // group_size
    levels = lax.broadcasted_iota(jnp.int32, (1, LMAX), 1)
    onehot = (band_multipole[:, None] == levels).astype(jnp.float32)
    picked = jnp.dot(onehot, radial_weight, precision=lax.Precision.HIGHEST)
    weighted = (band_table.astype(jnp.float32) * picked * green_weight[:, None]).astype(
        jnp.bfloat16
    )
    gathered = lax.all_gather(weighted, "kpt", axis=0, tiled=True)
    band_total = gathered.shape[0]
    kernel_rows = build_part(left_table, gathered)
    shaped = kernel_rows.reshape(group_size, block_rows, band_total)
    relaid = lax.all_to_all(shaped, "kpt", split_axis=0, concat_axis=0, tiled=True)
    return relaid.reshape(row_count, band_total)


def grid_kernel(
    left, band, mult, radial, green, out,
    lbuf, bbuf, rbuf, info, infoin, infobuf, psend, precv, msg, outbuf,
    rsem, lsem, bsem, isem, psem, osem, lsend, bsend, isend, osend, know,
):
    e = lax.axis_index("energy")
    k = lax.axis_index("kpt")
    c, x, z = k % 2, (k // 2) % 2, k // 4
    half = lbuf.shape[1]
    step = half // CHUNKS
    rows = left.shape[0]
    own = k % 4

    barrier = pltpu.get_barrier_semaphore()
    across_y = (1 - e, k)
    for target in (
        [(e, 4 * ((z + dz) % 4) + 2 * x + e) for dz in (1, 2, 3)]
        + [(e, 4 * z + 2 * (1 - x) + dc) for dc in range(2)]
        + [(e, 4 * z + 2 * x + 1 - c), across_y]
    ):
        pl.semaphore_signal(barrier, inc=1, device_id=target, device_id_type=MESH)

    def cols(core, n):
        return pl.ds(pl.multiple_of(core * half + n * step, 128), step)

    def slot(i):
        return pl.ds(pl.multiple_of(i * rows, rows), rows)

    def at(n):
        return pl.ds(n * step, step)

    radial_copy = pltpu.make_async_copy(
        radial.at[:, pl.ds(pl.multiple_of(c * half, 128), half)], rbuf, rsem
    )
    radial_copy.start()
    for n in range(CHUNKS):
        pltpu.make_async_copy(
            left.at[:, cols(c, n)], lbuf.at[slot(own), at(n)], lsem.at[own, n]
        ).start()

    @pl.when(c == e)
    def _():
        for n in range(CHUNKS):
            pltpu.make_async_copy(
                band.at[:, cols(c, n)], bbuf.at[slot(z), at(n)], bsem.at[z, n]
            ).start()

    row = lax.broadcasted_iota(jnp.int32, info.shape, 0)
    info[...] = jnp.zeros_like(info)
    info[0:1, 0:rows] = green[...]
    info[1:2, 0:rows] = green[...]
    info[2:3, 0:rows] = mult[...].astype(jnp.float32)
    info[...] = pltpu.roll(info[...], z * rows, 1)

    @pl.when(c == e)
    def _():
        pl.semaphore_wait(barrier, 10)

    @pl.when(c != e)
    def _():
        pl.semaphore_wait(barrier, 4)

    info_over = pltpu.make_async_remote_copy(
        src_ref=info, dst_ref=infoin, send_sem=isend.at[7], recv_sem=isend.at[8],
        device_id=across_y, device_id_type=MESH,
    )

    @pl.when(c != e)
    def _():
        info_over.start()

    sends = []
    info_sends = [
        pltpu.make_async_remote_copy(
            src_ref=infobuf.at[z], dst_ref=infobuf.at[z], send_sem=isend.at[i],
            recv_sem=isem.at[z], device_id=(e, ((z + dz) % 4) * 4 + 2 * x + (c + dc) % 2),
            device_id_type=MESH,
        )
        for i, (dz, dc) in enumerate(((1, 0), (1, 1), (2, 0), (2, 1), (3, 0), (3, 1), (0, 1)))
    ]
    band_sends = []
    for n in range(CHUNKS):
        for i, (dx, dc) in enumerate(((1, 0), (1, 1), (0, 1))):
            core = (c + dc) % 2
            copy = pltpu.make_async_remote_copy(
                src_ref=left.at[:, cols(core, n)], dst_ref=lbuf.at[slot(own), at(n)],
                send_sem=lsend.at[i, n], recv_sem=lsem.at[own, n],
                device_id=(e, 4 * z + 2 * ((x + dx) % 2) + core), device_id_type=MESH,
            )
            copy.start()
            sends.append(copy)
        for i, (dz, dc) in enumerate(((1, 0), (1, 1), (2, 0), (2, 1), (3, 0), (3, 1), (0, 1))):
            core = (c + dc) % 2
            band_sends.append(
                pltpu.make_async_remote_copy(
                    src_ref=band.at[:, cols(core, n)], dst_ref=bbuf.at[slot(z), at(n)],
                    send_sem=bsend.at[i, n], recv_sem=bsem.at[z, n],
                    device_id=(e, ((z + dz) % 4) * 4 + 2 * x + core), device_id_type=MESH,
                )
            )

        @pl.when(c == e)
        def _():
            for copy in band_sends[n * 7:]:
                copy.start()
            if n == 0:
                info_over.wait_recv()
                infobuf[z] = jnp.where(row == 1 - e, infoin[...], info[...])
                for copy in info_sends:
                    copy.start()

    @pl.when(c == e)
    def _():
        pl.semaphore_signal(
            know, inc=1, device_id=(e, 4 * z + 2 * (1 - x) + c), device_id_type=MESH
        )
        pl.semaphore_wait(know, 1)
        pl.semaphore_signal(know, inc=1, device_id=across_y, device_id_type=MESH)

    radial_copy.wait()
    whole = rbuf[...]
    high = whole.astype(jnp.bfloat16)
    rest = whole - high.astype(jnp.float32)
    middle = rest.astype(jnp.bfloat16)
    low = rest - middle.astype(jnp.float32)
    terms = jnp.concatenate(
        [high.astype(jnp.float32), middle.astype(jnp.float32), low, jnp.zeros_like(low)], axis=0
    ).astype(jnp.bfloat16)

    for i in (1, 2, 3):
        other_z = (z + i) % 4
        pltpu.make_async_copy(info, infobuf.at[other_z], isem.at[other_z]).wait()

    @pl.when(c != e)
    def _():
        pltpu.make_async_copy(info, infobuf.at[z], isem.at[z]).wait()

    data = infobuf[0] + infobuf[1] + infobuf[2] + infobuf[3]
    lanes = 4 * rows
    down = lax.broadcasted_iota(jnp.int32, (lanes, lanes), 0)
    across = lax.broadcasted_iota(jnp.int32, (lanes, lanes), 1)
    scale = [
        jnp.sum(jnp.where(down == across, data[i:i + 1, :], 0.0), axis=1, keepdims=True)
        for i in range(2)
    ]
    first = c == 0
    mine = jnp.where(first, scale[0], scale[1])
    other = jnp.where(first, scale[1], scale[0])
    level = jnp.sum(jnp.where(down == across, data[2:3, :], 0.0), axis=1, keepdims=True)
    place = lax.broadcasted_iota(jnp.int32, (lanes, 4 * LMAX), 1)
    onehot = jnp.where(
        jnp.logical_and((place % LMAX).astype(jnp.float32) == level, place < 3 * LMAX), 1.0, 0.0
    ).astype(jnp.bfloat16)

    total = jnp.zeros((lanes, 2 * lanes), jnp.float32)
    for n in range(CHUNKS):
        picked = jnp.dot(
            onehot, terms[:, n * step:(n + 1) * step], preferred_element_type=jnp.float32
        )
        for i in range(4):
            pltpu.make_async_copy(
                lbuf.at[slot(i), at(n)], lbuf.at[slot(i), at(n)], lsem.at[i, n]
            ).wait()
            pltpu.make_async_copy(
                bbuf.at[slot(i), at(n)], bbuf.at[slot(i), at(n)], bsem.at[i, n]
            ).wait()
        product = bbuf[:, n * step:(n + 1) * step].astype(jnp.float32) * picked
        weighted = jnp.concatenate(
            [(product * other).astype(jnp.bfloat16), (product * mine).astype(jnp.bfloat16)], axis=0
        )
        total += lax.dot_general(
            lbuf[:, n * step:(n + 1) * step], weighted, (((1,), (1,)), ((), ())),
            preferred_element_type=jnp.float32,
        )

    psend[...] = total[:, :lanes]
    half_sum = pltpu.make_async_remote_copy(
        src_ref=psend, dst_ref=precv, send_sem=psem.at[0], recv_sem=psem.at[1],
        device_id=(e, 4 * z + 2 * x + (c + 1) % 2), device_id_type=MESH,
    )
    half_sum.start()
    block, pair = down // 8, down % 8
    order = jnp.where(across == (pair // 2) * rows + block * 2 + pair % 2, 1.0, 0.0).astype(
        jnp.bfloat16
    )
    half_sum.wait_recv()
    finished = (total[:, lanes:] + precv[...]).astype(jnp.bfloat16)
    cyclic = jnp.dot(order, finished, preferred_element_type=jnp.float32)
    msg[...] = cyclic.reshape(msg.shape)

    @pl.when(c != e)
    def _():
        pl.semaphore_wait(know, 1)

    for dq in range(16):
        q = (k + dq) % 16
        copy = pltpu.make_async_remote_copy(
            src_ref=msg.at[q], dst_ref=outbuf.at[z, 2 * x + e], send_sem=osend.at[dq],
            recv_sem=osem.at[z, 2 * x + e], device_id=(c, q), device_id_type=MESH,
        )
        if dq:
            copy.start()
            sends.append(copy)
        else:
            own_out = copy
    out_local = pltpu.make_async_copy(msg.at[k], outbuf.at[z, 2 * x + e], osem.at[z, 2 * x + e])

    @pl.when(c == e)
    def _():
        out_local.start()

    @pl.when(c != e)
    def _():
        own_out.start()

    lane = lax.broadcasted_iota(jnp.int32, (8, lanes), 1) // rows
    for zz in range(4):
        for s in range(4):
            pltpu.make_async_copy(msg.at[0], outbuf.at[zz, s], osem.at[zz, s]).wait()
    for top in range(2):
        for tile in range(4):
            parts = []
            for zz in (2 * top, 2 * top + 1):
                whole_tile = jnp.zeros((8, lanes), jnp.float32)
                for s in range(4):
                    turned = outbuf[zz, s]
                    if (s - tile) % 4:
                        turned = pltpu.roll(turned, ((s - tile) % 4) * rows, 1)
                    whole_tile = jnp.where(lane == s, turned, whole_tile)
                parts.append(whole_tile)
            out[top * 16:(top + 1) * 16, tile * lanes:(tile + 1) * lanes] = jnp.concatenate(
                parts, axis=0
            ).astype(jnp.bfloat16)

    for copy in sends:
        copy.wait_send()
    half_sum.wait_send()

    @pl.when(c == e)
    def _():
        for copy in band_sends + info_sends:
            copy.wait_send()

    @pl.when(c != e)
    def _():
        info_over.wait_send()
        own_out.wait_send()


def per_device_grid(left_table, band_table, band_multipole, radial_weight, green_weight):
    rows, points = left_table.shape
    lanes, half = 4 * rows, points // 2
    dma = pltpu.SemaphoreType.DMA
    any_space = pl.BlockSpec(memory_space=pl.ANY)
    vmem = pl.BlockSpec(memory_space=pltpu.VMEM)
    return pl.pallas_call(
        grid_kernel,
        out_shape=jax.ShapeDtypeStruct((rows, 16 * rows), jnp.bfloat16),
        in_specs=[any_space, any_space, vmem, any_space, vmem],
        out_specs=vmem,
        scratch_shapes=[
            pltpu.VMEM((lanes, half), jnp.bfloat16),
            pltpu.VMEM((lanes, half), jnp.bfloat16),
            pltpu.VMEM((LMAX, half), jnp.float32),
            pltpu.VMEM((8, lanes), jnp.float32),
            pltpu.VMEM((8, lanes), jnp.float32),
            pltpu.VMEM((4, 8, lanes), jnp.float32),
            pltpu.VMEM((lanes, lanes), jnp.float32),
            pltpu.VMEM((lanes, lanes), jnp.float32),
            pltpu.VMEM((16, 8, lanes), jnp.float32),
            pltpu.VMEM((4, 4, 8, lanes), jnp.float32),
            dma, dma((4, CHUNKS)), dma((4, CHUNKS)), dma((4,)), dma((2,)), dma((4, 4)),
            dma((3, CHUNKS)), dma((7, CHUNKS)), dma((9,)), dma((16,)),
            pltpu.SemaphoreType.REGULAR,
        ],
        compiler_params=pltpu.CompilerParams(
            collective_id=0, has_side_effects=True, vmem_limit_bytes=60 * 1024 * 1024
        ),
    )(left_table, band_table, band_multipole.reshape(1, rows), radial_weight, green_weight.reshape(1, rows))


def solution(mesh):
    in_specs = (P("kpt", None), P("kpt", None), P("kpt"), P(), P(("energy", "kpt")))
    out_specs = P(("energy", "kpt"), None)

    def step(left_table, band_table, band_multipole, radial_weight, green_weight):
        small = (
            mesh.shape["energy"] == 2
            and mesh.shape["kpt"] == 16
            and left_table.shape == band_table.shape == (32, 4096)
        )
        body = per_device_grid if small else per_device
        return body(left_table, band_table, band_multipole, radial_weight, green_weight)

    return jax.shard_map(
        step, mesh=mesh, in_specs=in_specs, out_specs=out_specs, check_vma=False
    )
```

```python
import functools

import jax
import jax.numpy as jnp
from jax import lax
from jax.experimental import pallas as pl
from jax.experimental.pallas import tpu as pltpu
from jax.sharding import PartitionSpec as P

LMAX = 8
MESH = pl.DeviceIdType.MESH
CHUNKS = 4
BAND_ORDER = ((2, 0), (2, 1), (1, 0), (1, 1), (3, 0), (3, 1), (0, 1))


def build_part(left_table, band_part):
    return lax.dot_general(
        left_table, band_part, (((1,), (1,)), ((), ())), preferred_element_type=jnp.float32
    ).astype(jnp.bfloat16)


def per_device(left_table, band_table, band_multipole, radial_weight, green_weight):
    group_size = lax.axis_size("kpt")
    row_count = left_table.shape[0]
    block_rows = row_count // group_size
    levels = lax.broadcasted_iota(jnp.int32, (1, LMAX), 1)
    onehot = (band_multipole[:, None] == levels).astype(jnp.float32)
    picked = jnp.dot(onehot, radial_weight, precision=lax.Precision.HIGHEST)
    weighted = (band_table.astype(jnp.float32) * picked * green_weight[:, None]).astype(
        jnp.bfloat16
    )
    gathered = lax.all_gather(weighted, "kpt", axis=0, tiled=True)
    band_total = gathered.shape[0]
    kernel_rows = build_part(left_table, gathered)
    shaped = kernel_rows.reshape(group_size, block_rows, band_total)
    relaid = lax.all_to_all(shaped, "kpt", split_axis=0, concat_axis=0, tiled=True)
    return relaid.reshape(row_count, band_total)


def grid_kernel(
    left, band, mult, radial, green, out,
    lbuf, bbuf, rbuf, info, infoin, infobuf, psend, precv, msg, outbuf,
    rsem, lsem, bsem, isem, psem, osem, lsend, bsend, isend, osend, fsend, know,
):
    e = lax.axis_index("energy")
    k = lax.axis_index("kpt")
    c, x, z = k % 2, (k // 2) % 2, k // 4
    half = lbuf.shape[1]
    step = half // CHUNKS
    rows = left.shape[0]
    own = k % 4

    barrier = pltpu.get_barrier_semaphore()
    across_y = (1 - e, k)
    for target in (
        [(e, 4 * ((z + dz) % 4) + 2 * x + e) for dz in (1, 2, 3)]
        + [(e, 4 * z + 2 * (1 - x) + dc) for dc in range(2)]
        + [(e, 4 * z + 2 * x + 1 - c), across_y]
    ):
        pl.semaphore_signal(barrier, inc=1, device_id=target, device_id_type=MESH)

    def cols(core, n):
        return pl.ds(pl.multiple_of(core * half + n * step, 128), step)

    def slot(i):
        return pl.ds(pl.multiple_of(i * rows, rows), rows)

    def at(n):
        return pl.ds(n * step, step)

    radial_copy = pltpu.make_async_copy(
        radial.at[:, pl.ds(pl.multiple_of(c * half, 128), half)], rbuf, rsem
    )
    radial_copy.start()
    for n in range(CHUNKS):
        pltpu.make_async_copy(
            left.at[:, cols(c, n)], lbuf.at[slot(own), at(n)], lsem.at[own, n]
        ).start()

    @pl.when(c == e)
    def _():
        for n in range(CHUNKS):
            pltpu.make_async_copy(
                band.at[:, cols(c, n)], bbuf.at[slot(z), at(n)], bsem.at[z, n]
            ).start()

    row = lax.broadcasted_iota(jnp.int32, info.shape, 0)
    info[...] = jnp.zeros_like(info)
    info[0:1, 0:rows] = green[...]
    info[1:2, 0:rows] = green[...]
    info[2:3, 0:rows] = mult[...].astype(jnp.float32)
    info[...] = pltpu.roll(info[...], z * rows, 1)

    @pl.when(c == e)
    def _():
        pl.semaphore_wait(barrier, 10)

    @pl.when(c != e)
    def _():
        pl.semaphore_wait(barrier, 4)

    info_over = pltpu.make_async_remote_copy(
        src_ref=info, dst_ref=infoin, send_sem=isend.at[7], recv_sem=isend.at[8],
        device_id=across_y, device_id_type=MESH,
    )

    @pl.when(c != e)
    def _():
        info_over.start()

    sends = []
    info_sends = [
        pltpu.make_async_remote_copy(
            src_ref=infobuf.at[z], dst_ref=infobuf.at[z], send_sem=isend.at[i],
            recv_sem=isem.at[z], device_id=(e, ((z + dz) % 4) * 4 + 2 * x + (c + dc) % 2),
            device_id_type=MESH,
        )
        for i, (dz, dc) in enumerate(((1, 0), (1, 1), (2, 0), (2, 1), (3, 0), (3, 1), (0, 1)))
    ]
    inner = jnp.logical_or(z == 1, z == 2)
    far = jnp.where(z >= 2, 0, 3)
    relays = [
        pltpu.make_async_remote_copy(
            src_ref=bbuf.at[slot(far), at(n)], dst_ref=bbuf.at[slot(far), at(n)],
            send_sem=fsend.at[n], recv_sem=bsem.at[far, n],
            device_id=(e, 4 * (3 - far) + 2 * x + c), device_id_type=MESH,
        )
        for n in range(CHUNKS)
    ]
    band_sends = []

    def direct(n, act):
        for copy, (dz, _) in zip(band_sends[n * 7:n * 7 + 7], BAND_ORDER):
            if dz in (0, 2):
                act(copy)
            else:
                pl.when(z != (3 if dz == 1 else 0))(functools.partial(act, copy))

    for n in range(CHUNKS):
        for i, (dx, dc) in enumerate(((1, 0), (1, 1), (0, 1))):
            core = (c + dc) % 2
            copy = pltpu.make_async_remote_copy(
                src_ref=left.at[:, cols(core, n)], dst_ref=lbuf.at[slot(own), at(n)],
                send_sem=lsend.at[i, n], recv_sem=lsem.at[own, n],
                device_id=(e, 4 * z + 2 * ((x + dx) % 2) + core), device_id_type=MESH,
            )
            copy.start()
            sends.append(copy)
        for i, (dz, dc) in enumerate(BAND_ORDER):
            core = (c + dc) % 2
            band_sends.append(
                pltpu.make_async_remote_copy(
                    src_ref=band.at[:, cols(core, n)], dst_ref=bbuf.at[slot(z), at(n)],
                    send_sem=bsend.at[i, n], recv_sem=bsem.at[z, n],
                    device_id=(e, ((z + dz) % 4) * 4 + 2 * x + core), device_id_type=MESH,
                )
            )

        @pl.when(c == e)
        def _():
            direct(n, lambda copy: copy.start())
            if n == 0:
                info_over.wait_recv()
                infobuf[z] = jnp.where(row == 1 - e, infoin[...], info[...])
                for copy in info_sends:
                    copy.start()

    @pl.when(c == e)
    def _():
        pl.semaphore_signal(
            know, inc=1, device_id=(e, 4 * z + 2 * (1 - x) + c), device_id_type=MESH
        )
        pl.semaphore_wait(know, 1)
        pl.semaphore_signal(know, inc=1, device_id=across_y, device_id_type=MESH)

    radial_copy.wait()
    whole = rbuf[...]
    high = whole.astype(jnp.bfloat16)
    rest = whole - high.astype(jnp.float32)
    middle = rest.astype(jnp.bfloat16)
    low = rest - middle.astype(jnp.float32)
    terms = jnp.concatenate(
        [high.astype(jnp.float32), middle.astype(jnp.float32), low, jnp.zeros_like(low)], axis=0
    ).astype(jnp.bfloat16)

    for i in (1, 2, 3):
        other_z = (z + i) % 4
        pltpu.make_async_copy(info, infobuf.at[other_z], isem.at[other_z]).wait()

    @pl.when(c != e)
    def _():
        pltpu.make_async_copy(info, infobuf.at[z], isem.at[z]).wait()

    data = infobuf[0] + infobuf[1] + infobuf[2] + infobuf[3]
    lanes = 4 * rows
    down = lax.broadcasted_iota(jnp.int32, (lanes, lanes), 0)
    across = lax.broadcasted_iota(jnp.int32, (lanes, lanes), 1)
    scale = [
        jnp.sum(jnp.where(down == across, data[i:i + 1, :], 0.0), axis=1, keepdims=True)
        for i in range(2)
    ]
    first = c == 0
    mine = jnp.where(first, scale[0], scale[1])
    other = jnp.where(first, scale[1], scale[0])
    level = jnp.sum(jnp.where(down == across, data[2:3, :], 0.0), axis=1, keepdims=True)
    place = lax.broadcasted_iota(jnp.int32, (lanes, 4 * LMAX), 1)
    onehot = jnp.where(
        jnp.logical_and((place % LMAX).astype(jnp.float32) == level, place < 3 * LMAX), 1.0, 0.0
    ).astype(jnp.bfloat16)

    def band_wait(i, n):
        pltpu.make_async_copy(
            bbuf.at[slot(i), at(n)], bbuf.at[slot(i), at(n)], bsem.at[i, n]
        ).wait()

    total = jnp.zeros((lanes, 2 * lanes), jnp.float32)
    for n in range(CHUNKS):
        picked = jnp.dot(
            onehot, terms[:, n * step:(n + 1) * step], preferred_element_type=jnp.float32
        )
        band_wait(far, n)
        pl.when(inner)(relays[n].start)
        for i in range(4):
            pltpu.make_async_copy(
                lbuf.at[slot(i), at(n)], lbuf.at[slot(i), at(n)], lsem.at[i, n]
            ).wait()
        for i in (1, 2, 3):
            band_wait((far + i) % 4, n)
        product = bbuf[:, n * step:(n + 1) * step].astype(jnp.float32) * picked
        weighted = jnp.concatenate(
            [(product * other).astype(jnp.bfloat16), (product * mine).astype(jnp.bfloat16)], axis=0
        )
        total += lax.dot_general(
            lbuf[:, n * step:(n + 1) * step], weighted, (((1,), (1,)), ((), ())),
            preferred_element_type=jnp.float32,
        )

    psend[...] = total[:, :lanes]
    half_sum = pltpu.make_async_remote_copy(
        src_ref=psend, dst_ref=precv, send_sem=psem.at[0], recv_sem=psem.at[1],
        device_id=(e, 4 * z + 2 * x + (c + 1) % 2), device_id_type=MESH,
    )
    half_sum.start()
    block, pair = down // 8, down % 8
    order = jnp.where(across == (pair // 2) * rows + block * 2 + pair % 2, 1.0, 0.0).astype(
        jnp.bfloat16
    )
    half_sum.wait_recv()
    finished = (total[:, lanes:] + precv[...]).astype(jnp.bfloat16)
    cyclic = jnp.dot(order, finished, preferred_element_type=jnp.float32)
    msg[...] = cyclic.reshape(msg.shape)

    @pl.when(c != e)
    def _():
        pl.semaphore_wait(know, 1)

    for dq in range(16):
        q = (k + dq) % 16
        copy = pltpu.make_async_remote_copy(
            src_ref=msg.at[q], dst_ref=outbuf.at[z, 2 * x + e], send_sem=osend.at[dq],
            recv_sem=osem.at[z, 2 * x + e], device_id=(c, q), device_id_type=MESH,
        )
        if dq:
            copy.start()
            sends.append(copy)
        else:
            own_out = copy
    out_local = pltpu.make_async_copy(msg.at[k], outbuf.at[z, 2 * x + e], osem.at[z, 2 * x + e])

    @pl.when(c == e)
    def _():
        out_local.start()

    @pl.when(c != e)
    def _():
        own_out.start()

    lane = lax.broadcasted_iota(jnp.int32, (8, lanes), 1) // rows
    for zz in range(4):
        for s in range(4):
            pltpu.make_async_copy(msg.at[0], outbuf.at[zz, s], osem.at[zz, s]).wait()
    for top in range(2):
        for tile in range(4):
            parts = []
            for zz in (2 * top, 2 * top + 1):
                whole_tile = jnp.zeros((8, lanes), jnp.float32)
                for s in range(4):
                    turned = outbuf[zz, s]
                    if (s - tile) % 4:
                        turned = pltpu.roll(turned, ((s - tile) % 4) * rows, 1)
                    whole_tile = jnp.where(lane == s, turned, whole_tile)
                parts.append(whole_tile)
            out[top * 16:(top + 1) * 16, tile * lanes:(tile + 1) * lanes] = jnp.concatenate(
                parts, axis=0
            ).astype(jnp.bfloat16)

    for copy in sends:
        copy.wait_send()
    half_sum.wait_send()

    @pl.when(c == e)
    def _():
        for copy in info_sends:
            copy.wait_send()
        for n in range(CHUNKS):
            direct(n, lambda copy: copy.wait_send())

    @pl.when(inner)
    def _():
        for copy in relays:
            copy.wait_send()

    @pl.when(c != e)
    def _():
        info_over.wait_send()
        own_out.wait_send()


def per_device_grid(left_table, band_table, band_multipole, radial_weight, green_weight):
    rows, points = left_table.shape
    lanes, half = 4 * rows, points // 2
    dma = pltpu.SemaphoreType.DMA
    any_space = pl.BlockSpec(memory_space=pl.ANY)
    vmem = pl.BlockSpec(memory_space=pltpu.VMEM)
    return pl.pallas_call(
        grid_kernel,
        out_shape=jax.ShapeDtypeStruct((rows, 16 * rows), jnp.bfloat16),
        in_specs=[any_space, any_space, vmem, any_space, vmem],
        out_specs=vmem,
        scratch_shapes=[
            pltpu.VMEM((lanes, half), jnp.bfloat16),
            pltpu.VMEM((lanes, half), jnp.bfloat16),
            pltpu.VMEM((LMAX, half), jnp.float32),
            pltpu.VMEM((8, lanes), jnp.float32),
            pltpu.VMEM((8, lanes), jnp.float32),
            pltpu.VMEM((4, 8, lanes), jnp.float32),
            pltpu.VMEM((lanes, lanes), jnp.float32),
            pltpu.VMEM((lanes, lanes), jnp.float32),
            pltpu.VMEM((16, 8, lanes), jnp.float32),
            pltpu.VMEM((4, 4, 8, lanes), jnp.float32),
            dma, dma((4, CHUNKS)), dma((4, CHUNKS)), dma((4,)), dma((2,)), dma((4, 4)),
            dma((3, CHUNKS)), dma((7, CHUNKS)), dma((9,)), dma((16,)), dma((CHUNKS,)),
            pltpu.SemaphoreType.REGULAR,
        ],
        compiler_params=pltpu.CompilerParams(
            collective_id=0, has_side_effects=True, vmem_limit_bytes=60 * 1024 * 1024
        ),
    )(left_table, band_table, band_multipole.reshape(1, rows), radial_weight, green_weight.reshape(1, rows))


def solution(mesh):
    in_specs = (P("kpt", None), P("kpt", None), P("kpt"), P(), P(("energy", "kpt")))
    out_specs = P(("energy", "kpt"), None)

    def step(left_table, band_table, band_multipole, radial_weight, green_weight):
        small = (
            mesh.shape["energy"] == 2
            and mesh.shape["kpt"] == 16
            and left_table.shape == band_table.shape == (32, 4096)
        )
        body = per_device_grid if small else per_device
        return body(left_table, band_table, band_multipole, radial_weight, green_weight)

    return jax.shard_map(
        step, mesh=mesh, in_specs=in_specs, out_specs=out_specs, check_vma=False
    )
```

```python
import functools

import jax
import jax.numpy as jnp
from jax import lax
from jax.experimental import pallas as pl
from jax.experimental.pallas import tpu as pltpu
from jax.sharding import PartitionSpec as P

LMAX = 8
MESH = pl.DeviceIdType.MESH
CHUNKS = 4
BAND_ORDER = ((2, 0), (2, 1), (1, 0), (1, 1), (3, 0), (3, 1), (0, 1))


def build_part(left_table, band_part):
    return lax.dot_general(
        left_table, band_part, (((1,), (1,)), ((), ())), preferred_element_type=jnp.float32
    ).astype(jnp.bfloat16)


def per_device(left_table, band_table, band_multipole, radial_weight, green_weight):
    group_size = lax.axis_size("kpt")
    row_count = left_table.shape[0]
    block_rows = row_count // group_size
    levels = lax.broadcasted_iota(jnp.int32, (1, LMAX), 1)
    onehot = (band_multipole[:, None] == levels).astype(jnp.float32)
    picked = jnp.dot(onehot, radial_weight, precision=lax.Precision.HIGHEST)
    weighted = (band_table.astype(jnp.float32) * picked * green_weight[:, None]).astype(
        jnp.bfloat16
    )
    gathered = lax.all_gather(weighted, "kpt", axis=0, tiled=True)
    band_total = gathered.shape[0]
    kernel_rows = build_part(left_table, gathered)
    shaped = kernel_rows.reshape(group_size, block_rows, band_total)
    relaid = lax.all_to_all(shaped, "kpt", split_axis=0, concat_axis=0, tiled=True)
    return relaid.reshape(row_count, band_total)


def grid_kernel(
    left, band, mult, radial, green, out,
    lbuf, bbuf, rbuf, info, infoin, infobuf, psend, precv, msg, outbuf,
    rsem, lsem, bsem, isem, psem, osem, lsend, bsend, isend, osend, fsend, know,
):
    e = lax.axis_index("energy")
    k = lax.axis_index("kpt")
    c, x, z = k % 2, (k // 2) % 2, k // 4
    half = lbuf.shape[1]
    step = half // CHUNKS
    rows = left.shape[0]
    own = k % 4

    barrier = pltpu.get_barrier_semaphore()
    across_y = (1 - e, k)
    inner = jnp.logical_or(z == 1, z == 2)
    far = jnp.where(z >= 2, 0, 3)

    def beside_ends(dz, act):
        if dz in (0, 2):
            act()
        else:
            pl.when(z != (3 if dz == 1 else 0))(act)

    for dz in (2, 1, 3):
        beside_ends(dz, functools.partial(
            pl.semaphore_signal, barrier, inc=1,
            device_id=(e, 4 * ((z + dz) % 4) + 2 * x + e), device_id_type=MESH,
        ))
    for target in (
        [(e, 4 * z + 2 * (1 - x) + dc) for dc in range(2)]
        + [(e, 4 * z + 2 * x + 1 - c), across_y]
    ):
        pl.semaphore_signal(barrier, inc=1, device_id=target, device_id_type=MESH)

    def cols(core, n):
        return pl.ds(pl.multiple_of(core * half + n * step, 128), step)

    def slot(i):
        return pl.ds(pl.multiple_of(i * rows, rows), rows)

    def at(n):
        return pl.ds(n * step, step)

    radial_copy = pltpu.make_async_copy(
        radial.at[:, pl.ds(pl.multiple_of(c * half, 128), half)], rbuf, rsem
    )
    radial_copy.start()
    for n in range(CHUNKS):
        pltpu.make_async_copy(
            left.at[:, cols(c, n)], lbuf.at[slot(own), at(n)], lsem.at[own, n]
        ).start()

    @pl.when(c == e)
    def _():
        for n in range(CHUNKS):
            pltpu.make_async_copy(
                band.at[:, cols(c, n)], bbuf.at[slot(z), at(n)], bsem.at[z, n]
            ).start()

    row = lax.broadcasted_iota(jnp.int32, info.shape, 0)
    info[...] = jnp.zeros_like(info)
    info[0:1, 0:rows] = green[...]
    info[1:2, 0:rows] = green[...]
    info[2:3, 0:rows] = mult[...].astype(jnp.float32)
    info[...] = pltpu.roll(info[...], z * rows, 1)

    @pl.when(jnp.logical_and(c == e, inner))
    def _():
        pl.semaphore_wait(barrier, 10)

    @pl.when(jnp.logical_and(c == e, jnp.logical_not(inner)))
    def _():
        pl.semaphore_wait(barrier, 8)

    @pl.when(c != e)
    def _():
        pl.semaphore_wait(barrier, 4)

    info_over = pltpu.make_async_remote_copy(
        src_ref=info, dst_ref=infoin, send_sem=isend.at[7], recv_sem=isend.at[8],
        device_id=across_y, device_id_type=MESH,
    )

    @pl.when(c != e)
    def _():
        info_over.start()

    sends = []
    info_sends = [
        pltpu.make_async_remote_copy(
            src_ref=infobuf.at[z], dst_ref=infobuf.at[z], send_sem=isend.at[i],
            recv_sem=isem.at[z], device_id=(e, ((z + dz) % 4) * 4 + 2 * x + (c + dc) % 2),
            device_id_type=MESH,
        )
        for i, (dz, dc) in enumerate(((1, 0), (1, 1), (2, 0), (2, 1), (3, 0), (3, 1), (0, 1)))
    ]
    info_relay = pltpu.make_async_remote_copy(
        src_ref=infobuf.at[far], dst_ref=infobuf.at[far], send_sem=isend.at[9],
        recv_sem=isem.at[far], device_id=(e, 4 * (3 - far) + 2 * x + c), device_id_type=MESH,
    )
    relays = [
        pltpu.make_async_remote_copy(
            src_ref=bbuf.at[slot(far), at(n)], dst_ref=bbuf.at[slot(far), at(n)],
            send_sem=fsend.at[n], recv_sem=bsem.at[far, n],
            device_id=(e, 4 * (3 - far) + 2 * x + c), device_id_type=MESH,
        )
        for n in range(CHUNKS)
    ]
    band_sends = []

    def direct(n, act):
        for copy, (dz, _) in zip(band_sends[n * 7:n * 7 + 7], BAND_ORDER):
            beside_ends(dz, functools.partial(act, copy))

    def tell(act):
        for copy, dz in zip(info_sends, (1, 1, 2, 2, 3, 3, 0)):
            beside_ends(dz, functools.partial(act, copy))

    for n in range(CHUNKS):
        for i, (dx, dc) in enumerate(((1, 0), (1, 1), (0, 1))):
            core = (c + dc) % 2
            copy = pltpu.make_async_remote_copy(
                src_ref=left.at[:, cols(core, n)], dst_ref=lbuf.at[slot(own), at(n)],
                send_sem=lsend.at[i, n], recv_sem=lsem.at[own, n],
                device_id=(e, 4 * z + 2 * ((x + dx) % 2) + core), device_id_type=MESH,
            )
            copy.start()
            sends.append(copy)
        for i, (dz, dc) in enumerate(BAND_ORDER):
            core = (c + dc) % 2
            band_sends.append(
                pltpu.make_async_remote_copy(
                    src_ref=band.at[:, cols(core, n)], dst_ref=bbuf.at[slot(z), at(n)],
                    send_sem=bsend.at[i, n], recv_sem=bsem.at[z, n],
                    device_id=(e, ((z + dz) % 4) * 4 + 2 * x + core), device_id_type=MESH,
                )
            )

        @pl.when(c == e)
        def _():
            direct(n, lambda copy: copy.start())
            if n == 0:
                info_over.wait_recv()
                infobuf[z] = jnp.where(row == 1 - e, infoin[...], info[...])
                tell(lambda copy: copy.start())

    radial_copy.wait()
    whole = rbuf[...]
    high = whole.astype(jnp.bfloat16)
    rest = whole - high.astype(jnp.float32)
    middle = rest.astype(jnp.bfloat16)
    low = rest - middle.astype(jnp.float32)
    terms = jnp.concatenate(
        [high.astype(jnp.float32), middle.astype(jnp.float32), low, jnp.zeros_like(low)], axis=0
    ).astype(jnp.bfloat16)

    def info_wait(i):
        pltpu.make_async_copy(info, infobuf.at[i], isem.at[i]).wait()

    @pl.when(c != e)
    def _():
        info_wait(z)

    info_wait(far)
    pl.when(inner)(info_relay.start)
    info_wait(jnp.where(inner, 3 - far, 1))
    info_wait(jnp.where(inner, 3 - z, 2))
    data = infobuf[0] + infobuf[1] + infobuf[2] + infobuf[3]
    lanes = 4 * rows
    down = lax.broadcasted_iota(jnp.int32, (lanes, lanes), 0)
    across = lax.broadcasted_iota(jnp.int32, (lanes, lanes), 1)
    scale = [
        jnp.sum(jnp.where(down == across, data[i:i + 1, :], 0.0), axis=1, keepdims=True)
        for i in range(2)
    ]
    first = c == 0
    mine = jnp.where(first, scale[0], scale[1])
    other = jnp.where(first, scale[1], scale[0])
    level = jnp.sum(jnp.where(down == across, data[2:3, :], 0.0), axis=1, keepdims=True)
    place = lax.broadcasted_iota(jnp.int32, (lanes, 4 * LMAX), 1)
    onehot = jnp.where(
        jnp.logical_and((place % LMAX).astype(jnp.float32) == level, place < 3 * LMAX), 1.0, 0.0
    ).astype(jnp.bfloat16)

    def band_wait(i, n):
        pltpu.make_async_copy(
            bbuf.at[slot(i), at(n)], bbuf.at[slot(i), at(n)], bsem.at[i, n]
        ).wait()

    total = jnp.zeros((lanes, 2 * lanes), jnp.float32)
    for n in range(CHUNKS):
        picked = jnp.dot(
            onehot, terms[:, n * step:(n + 1) * step], preferred_element_type=jnp.float32
        )
        band_wait(far, n)
        pl.when(inner)(relays[n].start)
        for i in range(4):
            pltpu.make_async_copy(
                lbuf.at[slot(i), at(n)], lbuf.at[slot(i), at(n)], lsem.at[i, n]
            ).wait()
        for i in (1, 2, 3):
            band_wait((far + i) % 4, n)
        if n == 0:
            @pl.when(c == e)
            def _():
                pl.semaphore_signal(
                    know, inc=1, device_id=(e, 4 * z + 2 * (1 - x) + c), device_id_type=MESH
                )
                pl.semaphore_wait(know, 1)
                pl.semaphore_signal(know, inc=1, device_id=across_y, device_id_type=MESH)

        product = bbuf[:, n * step:(n + 1) * step].astype(jnp.float32) * picked
        weighted = jnp.concatenate(
            [(product * other).astype(jnp.bfloat16), (product * mine).astype(jnp.bfloat16)], axis=0
        )
        total += lax.dot_general(
            lbuf[:, n * step:(n + 1) * step], weighted, (((1,), (1,)), ((), ())),
            preferred_element_type=jnp.float32,
        )

    psend[...] = total[:, :lanes]
    half_sum = pltpu.make_async_remote_copy(
        src_ref=psend, dst_ref=precv, send_sem=psem.at[0], recv_sem=psem.at[1],
        device_id=(e, 4 * z + 2 * x + (c + 1) % 2), device_id_type=MESH,
    )
    half_sum.start()
    block, pair = down // 8, down % 8
    order = jnp.where(across == (pair // 2) * rows + block * 2 + pair % 2, 1.0, 0.0).astype(
        jnp.bfloat16
    )
    half_sum.wait_recv()
    finished = (total[:, lanes:] + precv[...]).astype(jnp.bfloat16)
    cyclic = jnp.dot(order, finished, preferred_element_type=jnp.float32)
    msg[...] = cyclic.reshape(msg.shape)

    @pl.when(c != e)
    def _():
        pl.semaphore_wait(know, 1)

    for dq in range(16):
        q = (k + dq) % 16
        copy = pltpu.make_async_remote_copy(
            src_ref=msg.at[q], dst_ref=outbuf.at[z, 2 * x + e], send_sem=osend.at[dq],
            recv_sem=osem.at[z, 2 * x + e], device_id=(c, q), device_id_type=MESH,
        )
        if dq:
            copy.start()
            sends.append(copy)
        else:
            own_out = copy
    out_local = pltpu.make_async_copy(msg.at[k], outbuf.at[z, 2 * x + e], osem.at[z, 2 * x + e])

    @pl.when(c == e)
    def _():
        out_local.start()

    @pl.when(c != e)
    def _():
        own_out.start()

    lane = lax.broadcasted_iota(jnp.int32, (8, lanes), 1) // rows
    for zz in range(4):
        for s in range(4):
            pltpu.make_async_copy(msg.at[0], outbuf.at[zz, s], osem.at[zz, s]).wait()
    for top in range(2):
        for tile in range(4):
            parts = []
            for zz in (2 * top, 2 * top + 1):
                whole_tile = jnp.zeros((8, lanes), jnp.float32)
                for s in range(4):
                    turned = outbuf[zz, s]
                    if (s - tile) % 4:
                        turned = pltpu.roll(turned, ((s - tile) % 4) * rows, 1)
                    whole_tile = jnp.where(lane == s, turned, whole_tile)
                parts.append(whole_tile)
            out[top * 16:(top + 1) * 16, tile * lanes:(tile + 1) * lanes] = jnp.concatenate(
                parts, axis=0
            ).astype(jnp.bfloat16)

    for copy in sends:
        copy.wait_send()
    half_sum.wait_send()

    @pl.when(c == e)
    def _():
        tell(lambda copy: copy.wait_send())
        for n in range(CHUNKS):
            direct(n, lambda copy: copy.wait_send())

    @pl.when(inner)
    def _():
        info_relay.wait_send()
        for copy in relays:
            copy.wait_send()

    @pl.when(c != e)
    def _():
        info_over.wait_send()
        own_out.wait_send()


def per_device_grid(left_table, band_table, band_multipole, radial_weight, green_weight):
    rows, points = left_table.shape
    lanes, half = 4 * rows, points // 2
    dma = pltpu.SemaphoreType.DMA
    any_space = pl.BlockSpec(memory_space=pl.ANY)
    vmem = pl.BlockSpec(memory_space=pltpu.VMEM)
    return pl.pallas_call(
        grid_kernel,
        out_shape=jax.ShapeDtypeStruct((rows, 16 * rows), jnp.bfloat16),
        in_specs=[any_space, any_space, vmem, any_space, vmem],
        out_specs=vmem,
        scratch_shapes=[
            pltpu.VMEM((lanes, half), jnp.bfloat16),
            pltpu.VMEM((lanes, half), jnp.bfloat16),
            pltpu.VMEM((LMAX, half), jnp.float32),
            pltpu.VMEM((8, lanes), jnp.float32),
            pltpu.VMEM((8, lanes), jnp.float32),
            pltpu.VMEM((4, 8, lanes), jnp.float32),
            pltpu.VMEM((lanes, lanes), jnp.float32),
            pltpu.VMEM((lanes, lanes), jnp.float32),
            pltpu.VMEM((16, 8, lanes), jnp.float32),
            pltpu.VMEM((4, 4, 8, lanes), jnp.float32),
            dma, dma((4, CHUNKS)), dma((4, CHUNKS)), dma((4,)), dma((2,)), dma((4, 4)),
            dma((3, CHUNKS)), dma((7, CHUNKS)), dma((10,)), dma((16,)), dma((CHUNKS,)),
            pltpu.SemaphoreType.REGULAR,
        ],
        compiler_params=pltpu.CompilerParams(
            collective_id=0, has_side_effects=True, vmem_limit_bytes=60 * 1024 * 1024
        ),
    )(left_table, band_table, band_multipole.reshape(1, rows), radial_weight, green_weight.reshape(1, rows))


def solution(mesh):
    in_specs = (P("kpt", None), P("kpt", None), P("kpt"), P(), P(("energy", "kpt")))
    out_specs = P(("energy", "kpt"), None)

    def step(left_table, band_table, band_multipole, radial_weight, green_weight):
        small = (
            mesh.shape["energy"] == 2
            and mesh.shape["kpt"] == 16
            and left_table.shape == band_table.shape == (32, 4096)
        )
        body = per_device_grid if small else per_device
        return body(left_table, band_table, band_multipole, radial_weight, green_weight)

    return jax.shard_map(
        step, mesh=mesh, in_specs=in_specs, out_specs=out_specs, check_vma=False
    )
```
